768 devices in a mesh: pipe: 24 (over z_lo, y), dp: 32 (over z_hi, x, core).
Axes of the slice: x: 4, y: 8, z: 12 (z_hi: 4, z_lo: 3; z = z_hi * 3 + z_lo), core: 2. Of those that a mesh axis runs over, the one named last changes fastest.
Arguments:
- hidden: bfloat16 [192, 7168], P('dp'), may hold values from -48 to 48
- head_weight: bfloat16 [98304, 7168], P(('pipe', 'dp')), may hold values from -48 to 48
- token_ids: int32 [192], replicated, may hold values from 0 to 98303
- segment_ids: int32 [192], replicated, may hold values from 0 to 15, never falling along the last dimension, each value on 1 to 16 neighbouring positions
Outputs:
- row_grad: bfloat16 [192, 7168], P('dp')
- weight_grad: bfloat16 [98304, 7168], P(('pipe', 'dp'))
- target_rows: bfloat16 [192, 7168], P('dp')
- mean_loss: float32 [], replicated
The draws below stay inside these ranges and needn't reach their ends.
All inputs are finite; a program needn't handle non-finite values.
Results may differ from the reference program's by a relative error of at most 0.0049.
Values may be sent and summed in bfloat16 or wider, within the bound.
A program may use at most 64 MiB of HBM per device.

```python
import math
import jax
import jax.numpy as jnp
import numpy as np
from jax import lax

D = 7168
SEG_MOST = 16
TOKENS = 192
VOCAB = 98304
NSEG = 16


def row_noise(key, entries):
    return jax.vmap(lambda entry: jax.random.normal(jax.random.fold_in(key, entry), (D,), jnp.float32))(entries)


def draw_head_weight(key, part):
    noise = row_noise(key, jnp.arange(VOCAB, dtype=jnp.int32))
    values = noise * (3.0 / math.sqrt(D))
    return jnp.clip(values, -48.0, 48.0).astype(jnp.bfloat16)


def draw_hidden(key, part):
    key = jax.random.fold_in(key, 9)
    values = jax.random.normal(key, (TOKENS, D), jnp.float32)
    return jnp.clip(values, -48.0, 48.0).astype(jnp.bfloat16)


def plant(result, rng, least, top_value):
    spot = [jax.random.randint(jax.random.fold_in(rng, axis), (), 0, length) for axis, length in enumerate(result.shape)]
    main_axis = result.shape.index(max(result.shape))
    beside = spot[:main_axis] + [(spot[main_axis] + 1) % result.shape[main_axis]] + spot[main_axis + 1:]
    return result.at[tuple(spot)].set(least).at[tuple(beside)].set(top_value)


def ranked_wide(rng, shape, amount, skew):
    portions = [min(1 << octave, amount + 1 - (1 << octave)) * (1 << 20) // math.isqrt((1 << octave) ** skew) + 1 for octave in range((amount + 1).bit_length()) if 1 << octave <= amount]
    deviation = 1 + sum(portions) // (1 << 30)
    grid = np.cumsum(np.array([max(1, weight // deviation) for weight in portions]))
    ticket = jax.random.randint(jax.random.fold_in(rng, 1), shape, 0, int(grid[len(portions) - 1]))
    start = jnp.left_shift(1, jnp.searchsorted(jnp.asarray(grid, jnp.int32), ticket, side="right").astype(jnp.int32))
    standing = start - 1 + jax.random.randint(jax.random.fold_in(rng, 4), shape, 0, 1 << 30) % jnp.minimum(start, amount + 1 - start)
    return jax.random.permutation(jax.random.fold_in(rng, 2), amount)[standing].astype(jnp.int32)


def split_up(amount, total, limit, skew):
    loads = [(1 << 20) // math.isqrt(standing ** skew) + 1 for standing in range(2, amount + 1)]
    rest, given = total - limit - (amount - 1), [1] * (amount - 1)
    while rest > 0:
        candidates = [i for i in range(amount - 1) if given[i] < limit]
        pool, remaining = sum([loads[i] for i in candidates]), rest
        for i in candidates:
            addition = min(limit - given[i], max(1, remaining * loads[i] // pool), rest)
            given[i] = given[i] + addition
            rest = rest - addition
    return np.array([limit] + given)


def uneven_parts(stream_key, count, total, bound, lean):
    if count == 2:
        one = jax.random.randint(stream_key, (), max(1, total - bound), min(bound, total - 1) + 1)
        return jnp.stack([one, total - one])
    tallies = jnp.asarray(split_up(count, total, bound, lean), jnp.int32)
    twos = (count - 1) // 2
    donor, sink = tallies[1:1 + 2 * twos:2], tallies[2:2 + 2 * twos:2]
    margin = jnp.minimum(donor - 1, bound - sink)
    shifted = jax.random.randint(jax.random.fold_in(stream_key, 1), (twos,), 0, 1 << 20) % (margin + 1)
    tallies = tallies.at[1:1 + 2 * twos:2].set(donor - shifted).at[2:2 + 2 * twos:2].set(sink + shifted)
    return tallies[jax.random.permutation(jax.random.fold_in(stream_key, 2), count)]


def setup_inputs(seed: int = 0) -> dict:
    streams_of = jax.random.split(jax.random.key(seed), 5)
    return {
        "hidden": draw_hidden(jax.random.fold_in(streams_of[4], 71), 0),
        "head_weight": draw_head_weight(jax.random.fold_in(streams_of[4], 71), 0),
        "token_ids": plant(ranked_wide(streams_of[2], (TOKENS,), VOCAB, 1), jax.random.fold_in(streams_of[2], 3), 0, VOCAB - 1).astype(jnp.int32),
        "segment_ids": jnp.searchsorted(jnp.cumsum(uneven_parts(streams_of[3], NSEG, TOKENS, SEG_MOST, 0)), jnp.arange(TOKENS), side="right").astype(jnp.int32),
    }


LOSS_SCALE = 4096.0


def token_weights(token_ids, segment_ids, turn_count):
    ahead_ids = jnp.concatenate([token_ids[2:], jnp.zeros((2,), jnp.int32)])
    ahead_segment = jnp.concatenate([segment_ids[2:], jnp.full((2,), -1, jnp.int32)])
    is_valid = (ahead_segment == segment_ids).astype(jnp.float32)
    member = (segment_ids[:, None] == jnp.arange(turn_count, dtype=jnp.int32)[None, :]).astype(jnp.float32)
    counts = jnp.sum(member * is_valid[:, None], axis=0)
    per_token = jnp.sum(member * counts[None, :], axis=1)
    weight = is_valid / (jnp.maximum(per_token, 1.0) * turn_count)
    return ahead_ids, weight


def reference(hidden, head_weight, token_ids, segment_ids):
    ahead_ids, weight = token_weights(token_ids, segment_ids, NSEG)
    logits = lax.dot_general(hidden, head_weight, (((1,), (1,)), ((), ())), preferred_element_type=jnp.float32)
    target_hit = ahead_ids[:, None] == jnp.arange(VOCAB, dtype=jnp.int32)[None, :]
    row_peak = jnp.max(logits, axis=1)
    log_total = row_peak + jnp.log(jnp.sum(jnp.exp(logits - row_peak[:, None]), axis=1))
    picked = jnp.sum(jnp.where(target_hit, logits, 0.0), axis=1)
    mean_loss = jnp.sum(weight * (log_total - picked))
    scaled = LOSS_SCALE * weight[:, None]
    probs = jnp.exp(logits - log_total[:, None])
    logit_grads = (scaled * (probs - target_hit.astype(jnp.float32))).astype(jnp.bfloat16)
    prob_grads = (scaled * probs).astype(jnp.bfloat16)
    row_grad = jnp.dot(logit_grads, head_weight, preferred_element_type=jnp.float32).astype(jnp.bfloat16)
    weight_grad = lax.dot_general(prob_grads, hidden, (((0,), (0,)), ((), ())), preferred_element_type=jnp.float32).astype(jnp.bfloat16)
    target_rows = (-scaled * hidden.astype(jnp.float32)).astype(jnp.bfloat16)
    return row_grad, weight_grad, target_rows, mean_loss
```

```python
import functools

import jax
import jax.numpy as jnp
import numpy as np
from jax import lax
from jax.experimental import pallas as pl
from jax.experimental.pallas import tpu as pltpu
from jax.sharding import PartitionSpec as P

MESH = pl.DeviceIdType.MESH
LOSS_SCALE = 4096.0
TURNS = 16
TOKENS = 192
WIDTH = 7168
PIECE = 896
VROWS = 128
BF16 = jnp.bfloat16
F32 = jnp.float32


def permutation():
    perm = np.zeros((TOKENS, TOKENS), np.float32)
    for j in range(8):
        for h in range(4):
            for r in range(6):
                perm[j * 24 + h * 6 + r, h * 48 + j * 6 + r] = 1.0
    return perm


def kernel(
    hid, w_ref, ids, perm_ref,
    rowg, wgrad, trow, loss,
    s1buf, scr48, hp, wg, acc, e_own, st, stx, sty, stz, eb, lgb, pf, pb, r1, r2s, r2, gs, gb, rowf, wgs,
    s1s, s1r, ws, wr, zs, zr, ys, yr, cs, cr, xs, xr, es, er, tys, tyr, tzs, tzr,
    r1ss, r1rs, r2ss, r2rs, gss, grs, outsem,
):
    pipe, dp = lax.axis_index("pipe"), lax.axis_index("dp")
    lo, y = pipe // 8, lax.rem(pipe, 8)
    h, j = dp // 8, lax.rem(dp, 8)
    x, c = j // 2, lax.rem(j, 2)
    z = h * 3 + lo
    cstar = h // 2

    def dev(jj, yy, zz):
        return (lax.rem(zz, 3) * 8 + yy, (zz // 3) * 8 + jj)

    sends = []

    def send(src, dst, ss, rs, to, cond=None):
        d = pltpu.make_async_remote_copy(
            src_ref=src, dst_ref=dst, send_sem=ss, recv_sem=rs, device_id=to, device_id_type=MESH
        )
        if cond is None:
            d.start()
        else:
            pl.when(cond)(d.start)
        sends.append((d, cond))

    def recv(dst, ss, rs, cond=None):
        d = pltpu.make_async_remote_copy(
            src_ref=dst, dst_ref=dst, send_sem=ss, recv_sem=rs,
            device_id=dev(j, lax.rem(y + 1, 8), z), device_id_type=MESH,
        )
        if cond is None:
            d.wait_recv()
        else:
            pl.when(cond)(d.wait_recv)

    bar = pltpu.get_barrier_semaphore()

    def hello(to):
        pl.semaphore_signal(bar, inc=1, device_id=to, device_id_type=MESH)

    for dj in range(1, 8):
        hello(dev(lax.rem(j + dj, 8), y, z))
    for dy in range(1, 8):
        hello(dev(j, lax.rem(y + dy, 8), z))
    for dz in range(1, 12):
        hello(dev(j, y, lax.rem(z + dz, 12)))
    for l3 in range(3):
        for jj in range(8):
            to = dev(jj, j, h * 3 + l3)
            if_other = jnp.logical_or(jnp.logical_or(j != y, jj != j), lo != l3)
            pl.when(if_other)(functools.partial(hello, to))
    pl.semaphore_wait(bar, 25 + 24 - (j == y).astype(jnp.int32))

    col = pl.ds(pl.multiple_of(y * PIECE, 128), PIECE)
    for dx in range(4):
        tx = lax.rem(x + dx, 4)
        send(
            hid.at[:, col], s1buf.at[j], s1s.at[dx], s1r.at[j], dev(tx * 2 + cstar, y, z),
            (c != cstar) if dx == 0 else None,
        )
    for dj in range(1, 8):
        tj = lax.rem(j + dj, 8)
        send(
            w_ref.at[:, pl.ds(pl.multiple_of(tj * PIECE, 128), PIECE)], wg.at[j],
            ws.at[dj], wr.at[j], dev(tj, y, z),
        )
    wg[j] = w_ref[:, pl.ds(pl.multiple_of(j * PIECE, 128), PIECE)]

    tok_ahead = ids[0:1, :]
    seg = ids[1:2, :]
    seg_ahead = ids[2:3, :]
    valid = (seg_ahead == seg).astype(F32)
    member = (lax.broadcasted_iota(jnp.int32, (TURNS, TOKENS), 0) == seg).astype(F32)
    counts = jnp.sum(member * valid, axis=1, keepdims=True)
    per_token = jnp.sum(member * counts, axis=0, keepdims=True)
    weight = valid / (jnp.maximum(per_token, 1.0) * TURNS)
    scaled = LOSS_SCALE * weight
    pick6 = (
        lax.broadcasted_iota(jnp.int32, (6, TOKENS), 1)
        == lax.broadcasted_iota(jnp.int32, (6, TOKENS), 0) + dp * 6
    )
    own_scaled = jnp.sum(jnp.where(pick6, scaled, 0.0), axis=1, keepdims=True)
    trow[...] = (-own_scaled * hid[...].astype(F32)).astype(BF16)

    @pl.when(c == cstar)
    def _():
        s1buf[j] = hid[:, col]
        for jj in range(8):
            recv(s1buf.at[jj], s1s.at[0], s1r.at[jj], jj != j)
        for jj in range(8):
            scr48[6 * jj:6 * jj + 6, :] = s1buf[jj].astype(F32)
        hp[y, h] = scr48[...].astype(BF16)

    for k in range(1, 4):
        send(hp.at[y, h], hp.at[y, h], zs.at[k], zr.at[k], dev(j, y, lax.rem(z + 3 * k, 12)), c == cstar)

    up, down = dev(j, lax.rem(y + 1, 8), z), dev(j, lax.rem(y + 7, 8), z)
    sib = dev(x * 2 + 1 - c, y, z)

    def ring_valid(k, way, s):
        return k <= 3 or (k == 4 and way == s)

    def slot(k, way):
        return 0 if k == 0 else (7 if k == 4 else 1 + 2 * (k - 1) + way)

    def piece(k, way):
        return y if k == 0 else lax.rem(y + (8 - k if way == 0 else k), 8)

    def pass_on(k, way, s):
        blk = hp.at[piece(k, way), 2 * c + s]
        for w in (0, 1):
            if (k == 0 or w == way) and ring_valid(k + 1, w, s):
                send(blk, blk, ys.at[w, s, k], yr.at[w, s, k], up if w == 0 else down)
        send(blk, blk, cs.at[slot(k, way), s], cr.at[slot(k, way), s], sib)

    def logits_of(k, way):
        p = piece(k, way)
        for s in range(2):
            blk = hp.at[p, 2 * (1 - c) + s]
            recv(blk, cs.at[slot(k, way), s], cr.at[slot(k, way), s])
        tile = w_ref[:, pl.ds(pl.multiple_of(p * PIECE, 128), PIECE)]
        tokens = hp[p].reshape(TOKENS, PIECE)
        part = lax.dot_general(tile, tokens, (((1,), (1,)), ((), ())), preferred_element_type=F32)
        if k == 0:
            acc[...] = part
        else:
            acc[...] += part

    for s in range(2):
        for k in range(1, 4):
            src_h = lax.rem(h + 4 - k, 4)
            recv(hp.at[y, src_h], zs.at[k], zr.at[k], src_h == 2 * c + s)
        pass_on(0, 0, s)
    for k in range(1, 5):
        for s in range(2):
            for way in range(2):
                if ring_valid(k, way, s):
                    blk = hp.at[piece(k, way), 2 * c + s]
                    recv(blk, ys.at[way, s, k - 1], yr.at[way, s, k - 1])
                    pass_on(k, way, s)
        logits_of(k - 1, 0)
        if k > 1:
            logits_of(k - 1, 1)
    logits_of(4, 0)

    logits = acc[...]
    vocab0 = (pipe * 32 + dp) * VROWS
    hit = lax.broadcasted_iota(jnp.int32, (VROWS, TOKENS), 0) == tok_ahead - vocab0
    peak = jnp.max(logits, axis=0, keepdims=True)
    ex = jnp.exp(logits - peak)
    total = jnp.sum(ex, axis=0, keepdims=True)
    picked = jnp.sum(jnp.where(hit, logits, 0.0), axis=0, keepdims=True)
    e_own[...] = ex

    def merge(buf, n):
        m = buf[0, 0:1, :]
        for i in range(1, n):
            m = jnp.maximum(m, buf[i, 0:1, :])
        s, p = jnp.zeros_like(m), jnp.zeros_like(m)
        for i in range(n):
            s += buf[i, 1:2, :] * jnp.exp(buf[i, 0:1, :] - m)
            p += buf[i, 2:3, :]
        return m, s, p

    def put(buf, idx, m, s, p):
        buf[idx, 0:1, :] = m
        buf[idx, 1:2, :] = s
        buf[idx, 2:3, :] = p
        buf[idx, 3:8, :] = jnp.zeros((5, TOKENS), F32)

    put(stx, j, peak, total, picked)
    for dj in range(1, 8):
        send(stx.at[j], stx.at[j], xs.at[dj], xr.at[j], dev(lax.rem(j + dj, 8), y, z))
    eb[j] = lax.dot_general(
        perm_ref[...].astype(BF16), ex.astype(BF16), (((1,), (1,)), ((), ())), preferred_element_type=F32
    ).astype(BF16)
    for dj in range(1, 8):
        send(eb.at[j], eb.at[j], es.at[dj], er.at[j], dev(lax.rem(j + dj, 8), y, z))

    for jj in range(8):
        recv(stx.at[jj], xs.at[0], xr.at[jj], jj != j)
    put(sty, y, *merge(stx, 8))
    for dy in range(1, 8):
        send(sty.at[y], sty.at[y], tys.at[dy], tyr.at[y], dev(j, lax.rem(y + dy, 8), z))
    for yy in range(8):
        recv(sty.at[yy], tys.at[0], tyr.at[yy], yy != y)
    put(stz, z, *merge(sty, 8))
    for dz in range(1, 12):
        send(stz.at[z], stz.at[z], tzs.at[dz], tzr.at[z], dev(j, y, lax.rem(z + dz, 12)))
    for zz in range(12):
        recv(stz.at[zz], tzs.at[0], tzr.at[zz], zz != z)
    m_all, s_all, p_all = merge(stz, 12)
    log_total = m_all + jnp.log(s_all)
    loss[...] = jnp.sum(weight * (log_total - p_all), axis=1, keepdims=True)

    for jj in range(8):
        st[jj:jj + 1, :] = scaled * jnp.exp(stx[jj, 0:1, :] - log_total)
    st[8:9, :] = scaled
    st[9:10, :] = tok_ahead.astype(F32)
    st[10:16, :] = jnp.zeros((6, TOKENS), F32)
    cols = lax.dot_general(
        perm_ref[...], st[...], (((1,), (1,)), ((), ())),
        preferred_element_type=F32, precision=lax.Precision.HIGHEST,
    )
    lane = lax.broadcasted_iota(jnp.int32, (TOKENS, VROWS), 1)
    ahead_col = jnp.round(cols[:, 9:10]).astype(jnp.int32)
    for jj in range(8):
        recv(eb.at[jj], es.at[0], er.at[jj], jj != j)
        vocab_j = (pipe * 32 + h * 8 + jj) * VROWS
        hit_j = lane == ahead_col - vocab_j
        lg = cols[:, jj:jj + 1] * eb[jj].astype(F32) - jnp.where(hit_j, cols[:, 8:9], 0.0)
        lgb[:, jj * VROWS:(jj + 1) * VROWS] = lg.astype(BF16)
    for jj in range(8):
        recv(wg.at[jj], ws.at[0], wr.at[jj], jj != j)
    part = jnp.dot(lgb[...], wg[...].reshape(8 * VROWS, PIECE), preferred_element_type=F32)
    pf[...] = part.reshape(8, 24, PIECE)
    pb[...] = pf[...].astype(BF16)

    for dy in range(1, 8):
        ty = lax.rem(y + dy, 8)
        send(pb.at[ty], r1.at[y], r1ss.at[dy], r1rs.at[y], dev(j, ty, z))

    probs = (scaled * (e_own[...] * jnp.exp(peak - log_total))).astype(BF16)
    for p in range(8):
        wgs[:, p * PIECE:(p + 1) * PIECE] = jnp.dot(
            probs, hp[p].reshape(TOKENS, PIECE), preferred_element_type=F32
        ).astype(BF16)
    out = pltpu.make_async_copy(wgs, wgrad, outsem)
    out.start()

    r1[y] = jnp.zeros((24, PIECE), BF16)
    tot = pf[y]
    for yy in range(8):
        recv(r1.at[yy], r1ss.at[0], r1rs.at[yy], yy != y)
        tot += r1[yy].astype(F32)
    for zz in range(12):
        r2s[zz] = tot[2 * zz:2 * zz + 2, :]
    for dz in range(1, 12):
        tz = lax.rem(z + dz, 12)
        send(r2s.at[tz], r2.at[z], r2ss.at[dz], r2rs.at[z], dev(j, y, tz))
    r2[z] = r2s[z]
    fin = jnp.zeros((2, PIECE), F32)
    for zz in range(12):
        recv(r2.at[zz], r2ss.at[0], r2rs.at[zz], zz != z)
        fin += r2[zz]
    gs[...] = fin.astype(BF16)

    for l3 in range(3):
        for yy in range(8):
            to = dev(y, yy, h * 3 + l3)
            other = jnp.logical_or(jnp.logical_or(j != y, yy != y), lo != l3)
            send(gs, gb.at[lo, j], gss.at[l3, yy], grs.at[lo, j], to, other)

    @pl.when(j == y)
    def _():
        gb[lo, j] = gs[...]

    for l3 in range(3):
        for jj in range(8):
            other = jnp.logical_or(jnp.logical_or(j != y, jj != j), lo != l3)
            recv(gb.at[l3, jj], gss.at[0, 0], grs.at[l3, jj], other)
            rowf[2 * l3:2 * l3 + 2, jj * PIECE:(jj + 1) * PIECE] = gb[l3, jj].astype(F32)
    rowg[...] = rowf[0:6, :].astype(BF16)

    for d, cond in sends:
        if cond is None:
            d.wait_send()
        else:
            pl.when(cond)(d.wait_send)
    out.wait()


def body(hidden, head_weight, token_ids, segment_ids):
    zeros = jnp.zeros((2,), jnp.int32)
    ids = jnp.stack(
        [
            jnp.concatenate([token_ids[2:], zeros]),
            segment_ids,
            jnp.concatenate([segment_ids[2:], zeros - 1]),
        ]
        + [segment_ids] * 5
    )
    dma = pltpu.SemaphoreType.DMA
    vmem = pl.BlockSpec(memory_space=pltpu.VMEM)
    row_grad, weight_grad, target_rows, loss = pl.pallas_call(
        kernel,
        out_shape=(
            jax.ShapeDtypeStruct((6, WIDTH), BF16),
            jax.ShapeDtypeStruct((VROWS, WIDTH), BF16),
            jax.ShapeDtypeStruct((6, WIDTH), BF16),
            jax.ShapeDtypeStruct((1, 1), F32),
        ),
        in_specs=[vmem] * 4,
        out_specs=(vmem, pl.BlockSpec(memory_space=pl.ANY), vmem, vmem),
        scratch_shapes=[
            pltpu.VMEM((8, 6, PIECE), BF16),
            pltpu.VMEM((48, PIECE), F32),
            pltpu.VMEM((8, 4, 48, PIECE), BF16),
            pltpu.VMEM((8, VROWS, PIECE), BF16),
            pltpu.VMEM((VROWS, TOKENS), F32),
            pltpu.VMEM((VROWS, TOKENS), F32),
            pltpu.VMEM((16, TOKENS), F32),
            pltpu.VMEM((8, 8, TOKENS), F32),
            pltpu.VMEM((8, 8, TOKENS), F32),
            pltpu.VMEM((12, 8, TOKENS), F32),
            pltpu.VMEM((8, TOKENS, VROWS), BF16),
            pltpu.VMEM((TOKENS, 8 * VROWS), BF16),
            pltpu.VMEM((8, 24, PIECE), F32),
            pltpu.VMEM((8, 24, PIECE), BF16),
            pltpu.VMEM((8, 24, PIECE), BF16),
            pltpu.VMEM((12, 2, PIECE), F32),
            pltpu.VMEM((12, 2, PIECE), F32),
            pltpu.VMEM((2, PIECE), BF16),
            pltpu.VMEM((3, 8, 2, PIECE), BF16),
            pltpu.VMEM((8, WIDTH), F32),
            pltpu.VMEM((VROWS, WIDTH), BF16),
            dma((4,)), dma((8,)), dma((8,)), dma((8,)), dma((4,)), dma((4,)),
            dma((2, 2, 4)), dma((2, 2, 4)), dma((8, 2)), dma((8, 2)),
            dma((8,)), dma((8,)), dma((8,)), dma((8,)), dma((8,)), dma((8,)), dma((12,)), dma((12,)),
            dma((8,)), dma((8,)), dma((12,)), dma((12,)), dma((3, 8)), dma((3, 8)), dma,
        ],
        compiler_params=pltpu.CompilerParams(
            collective_id=0, has_side_effects=True, vmem_limit_bytes=40 * 2**20
        ),
    )(hidden, head_weight, ids, jnp.asarray(permutation()))
    return (row_grad, weight_grad, target_rows, loss.reshape(()))


def solution(mesh):
    placed = (P("dp", None), P(("pipe", "dp"), None), P(), P())
    return jax.shard_map(
        body,
        mesh=mesh,
        in_specs=placed,
        out_specs=(P("dp", None), P(("pipe", "dp"), None), P("dp", None), P()),
        check_vma=False,
    )
```

```python
import functools

import jax
import jax.numpy as jnp
from jax import lax
from jax.experimental import pallas as pl
from jax.experimental.pallas import tpu as pltpu
from jax.sharding import PartitionSpec as P

MESH = pl.DeviceIdType.MESH
LOSS_SCALE = 4096.0
TURNS = 16
TOKENS = 192
WIDTH = 7168
PIECE = 896
VROWS = 128
BF16 = jnp.bfloat16
F32 = jnp.float32


def kernel(
    hid, w_hbm, tok_in, seg_in,
    rowg, wgrad, trow, loss,
    hidv, w_ref, sbuf, scr48, hp, wg, acc, e_own, st, stx, sty, stz, eb, lgb, pf, pb, hb, r1, rh, hsum, h2s, h2,
    r2s, r2, gs, gb, rowf, wgs,
    lsem, ss0, ss1, sr, ws, wr, ys, yr, zus, zds, zr, cs, cr, xs, xr, es, er, tys, tyr, tzs, tzr,
    r1ss, r1rs, rhss, rhrs, h2ss, h2rs, r2ss, r2rs, gss, grs, outsem,
):
    pipe, dp = lax.axis_index("pipe"), lax.axis_index("dp")
    lo, y = pipe // 8, lax.rem(pipe, 8)
    h, j = dp // 8, lax.rem(dp, 8)
    x, c = j // 2, lax.rem(j, 2)
    z = h * 3 + lo

    def dev(jj, yy, zz):
        return (lax.rem(zz, 3) * 8 + yy, (zz // 3) * 8 + jj)

    sends = []

    def send(src, dst, ss, rs, to, cond=None):
        d = pltpu.make_async_remote_copy(
            src_ref=src, dst_ref=dst, send_sem=ss, recv_sem=rs, device_id=to, device_id_type=MESH
        )
        if cond is None:
            d.start()
        else:
            pl.when(cond)(d.start)
        sends.append((d, cond))

    def recv(dst, ss, rs, cond=None):
        d = pltpu.make_async_remote_copy(
            src_ref=dst, dst_ref=dst, send_sem=ss, recv_sem=rs,
            device_id=dev(j, lax.rem(y + 1, 8), z), device_id_type=MESH,
        )
        if cond is None:
            d.wait_recv()
        else:
            pl.when(cond)(d.wait_recv)

    loads = [
        pltpu.make_async_copy(a, b, lsem.at[i])
        for i, (a, b) in enumerate(((hid, hidv), (w_hbm, w_ref)))
    ]
    bar = pltpu.get_barrier_semaphore()

    def hello(to):
        pl.semaphore_signal(bar, inc=1, device_id=to, device_id_type=MESH)

    for dz in (6, 5, 7, 4, 8, 3, 9, 2, 10, 1, 11):
        hello(dev(j, y, lax.rem(z + dz, 12)))
    for dy in (4, 3, 5, 2, 6, 1, 7):
        hello(dev(j, lax.rem(y + dy, 8), z))
    for dj in range(1, 8):
        hello(dev(lax.rem(j + dj, 8), y, z))
    near_z = jnp.where(c == 0, lax.rem(z + 11, 12), lax.rem(z + 1, 12))
    for cc in range(2):
        hello(dev(x * 2 + cc, y, near_z))
    from_z = lax.rem(z + 3 + 3 * lo, 12)

    @pl.when(c == 1)
    def _():
        for jj in range(8):
            hello(dev(jj, y, from_z))

    for d in loads:
        d.start()

    pl.semaphore_wait(bar, 25 + 2 + 4)

    col = pl.ds(pl.multiple_of(y * PIECE, 128), PIECE)
    far_z = lax.rem(z + 9 - 3 * lo, 12)
    for dx in (2, 1, 3, 0):
        tx = lax.rem(x + dx, 4)
        send(hid.at[:, col], sbuf.at[j], ss1.at[dx], sr.at[j], dev(tx * 2 + 1, y, far_z))
    for dx in (2, 1, 3, 0):
        tx = lax.rem(x + dx, 4)
        send(
            hid.at[:, col], sbuf.at[j], ss0.at[dx], sr.at[j], dev(tx * 2, y, z),
            (c != 0) if dx == 0 else None,
        )

    def send_w(dj):
        tj = lax.rem(j + dj, 8)
        send(
            w_hbm.at[:, pl.ds(pl.multiple_of(tj * PIECE, 128), PIECE)], wg.at[j],
            ws.at[dj], wr.at[j], dev(tj, y, z),
        )

    def shifted(v, fill):
        return jnp.concatenate([v[:, 2:], jnp.full((1, 2), fill, jnp.int32)], axis=1)

    tok_ahead = shifted(tok_in[...], 0)
    seg = seg_in[...]
    seg_ahead = shifted(seg, -1)
    valid = (seg_ahead == seg).astype(F32)
    member = (lax.broadcasted_iota(jnp.int32, (TURNS, TOKENS), 0) == seg).astype(F32)
    counts = jnp.sum(member * valid, axis=1, keepdims=True)
    per_token = jnp.sum(member * counts, axis=0, keepdims=True)
    weight = valid / (jnp.maximum(per_token, 1.0) * TURNS)
    scaled = LOSS_SCALE * weight
    pick6 = (
        lax.broadcasted_iota(jnp.int32, (6, TOKENS), 1)
        == lax.broadcasted_iota(jnp.int32, (6, TOKENS), 0) + dp * 6
    )
    own_scaled = jnp.sum(jnp.where(pick6, scaled, 0.0), axis=1, keepdims=True)
    row = lax.broadcasted_iota(jnp.int32, (TOKENS, TOKENS), 0)
    six = lax.shift_right_logical(row * 10923, 16)
    token_of = (six & 3) * 48 + lax.shift_right_logical(six, 2) * 6 + (row - six * 6)
    perm = (lax.broadcasted_iota(jnp.int32, (TOKENS, TOKENS), 1) == token_of).astype(F32)

    def columns(rows, order=perm):
        return lax.dot_general(
            order, rows, (((1,), (1,)), ((), ())),
            preferred_element_type=F32, precision=lax.Precision.HIGHEST,
        )

    st[0:8, :] = jnp.broadcast_to(tok_ahead.astype(F32), (8, TOKENS))
    zed = lax.shift_right_logical(row, 4)
    third = lax.shift_right_logical(zed * 21846, 16)
    token_of = third * 48 + (lax.shift_right_logical(row, 1) & 7) * 6 + (zed - third * 3) * 2 + (row & 1)
    order = (lax.broadcasted_iota(jnp.int32, (TOKENS, TOKENS), 1) == token_of).astype(F32)
    ahead_col = jnp.round(columns(st[0:8, :], order)[:, 0:1]).astype(jnp.int32)
    loads[0].wait()
    trow[...] = (-own_scaled * hidv[...].astype(F32)).astype(BF16)

    loads[1].wait()
    wg[j] = w_ref[:, pl.ds(pl.multiple_of(j * PIECE, 128), PIECE)]

    @pl.when(c == 0)
    def _():
        sbuf[j] = hidv[:, col]

    for jj in range(8):
        recv(sbuf.at[jj], ss0.at[0], sr.at[jj], jnp.logical_or(jj != j, c == 1))
    for jj in range(8):
        scr48[6 * jj:6 * jj + 6, :] = sbuf[jj].astype(F32)
    ring_of = (h, lax.rem(h + 1 + lo, 4))
    zed_of = (
        lax.rem(h + jnp.where(lo == 0, 3, lo), 4),
        lax.rem(h + jnp.where(lo == 2, 1, lo + 2), 4),
    )

    def mine(pair):
        return jnp.where(c == 0, pair[0], pair[1])

    def other(pair):
        return jnp.where(c == 0, pair[1], pair[0])

    ring_b, zed_b, sib_ring, sib_zed = mine(ring_of), mine(zed_of), other(ring_of), other(zed_of)
    hp[y, ring_b] = scr48[...].astype(BF16)

    right, left = dev(j, lax.rem(y + 1, 8), z), dev(j, lax.rem(y + 7, 8), z)
    above, below = dev(x * 2, y, lax.rem(z + 1, 12)), dev(x * 2 + 1, y, lax.rem(z + 11, 12))
    sib = dev(x * 2 + 1 - c, y, z)
    sends_up = c == jnp.where(lo < 2, 1, 0)
    sends_down = c == jnp.where(lo > 0, 1, 0)

    def slot(k, way):
        return 0 if k == 0 else (7 if k == 4 else 1 + 2 * (k - 1) + way)

    def piece(k, way):
        return y if k == 0 else lax.rem(y + (8 - k if way == 0 else k), 8)

    def pass_on(k, way):
        n = slot(k, way)
        blk = hp.at[piece(k, way), ring_b]
        for w in (0, 1):
            if (k == 0 or w == way) and k < 4:
                send(
                    blk, blk, ys.at[w, k], yr.at[w, k], right if w == 0 else left,
                    (c == w) if k == 3 else None,
                )
        send(blk, blk, zus.at[n], zr.at[n], above, sends_up)
        send(blk, blk, zds.at[n], zr.at[n], below, sends_down)
        send(blk, blk, cs.at[n, 0], cr.at[n, 0], sib)

    def zed_on(k, way):
        n = slot(k, way)
        blk = hp.at[piece(k, way), zed_b]
        recv(blk, zus.at[n], zr.at[n])
        send(blk, blk, cs.at[n, 1], cr.at[n, 1], sib)

    def logits_of(k, way):
        n, p = slot(k, way), piece(k, way)
        recv(hp.at[p, sib_ring], cs.at[n, 0], cr.at[n, 0])
        recv(hp.at[p, sib_zed], cs.at[n, 1], cr.at[n, 1])
        tile = w_ref[:, pl.ds(pl.multiple_of(p * PIECE, 128), PIECE)]
        tokens = hp[p].reshape(TOKENS, PIECE)
        part = lax.dot_general(tile, tokens, (((1,), (1,)), ((), ())), preferred_element_type=F32)
        if k == 0:
            acc[...] = part
        else:
            acc[...] += part

    def ways(k):
        return (0,) if k in (0, 4) else (0, 1)

    pass_on(0, 0)
    for dj in W_FIRST:
        send_w(dj)
    for k in range(1, 5):
        if k == 4:
            recv(hp.at[piece(4, 0), ring_b], ys.at[c, 3], yr.at[c, 3])
            pass_on(4, 0)
        else:
            for way in (0, 1):
                recv(hp.at[piece(k, way), ring_b], ys.at[way, k - 1], yr.at[way, k - 1])
                pass_on(k, way)
        for dj in W_LATER[k - 1]:
            send_w(dj)
        for way in ways(k - 1):
            zed_on(k - 1, way)
        if k >= 2:
            for way in ways(k - 2):
                logits_of(k - 2, way)
    zed_on(4, 0)
    for way in ways(3):
        logits_of(3, way)
    logits_of(4, 0)

    logits = acc[...]
    vocab0 = (pipe * 32 + dp) * VROWS
    hit = lax.broadcasted_iota(jnp.int32, (VROWS, TOKENS), 0) == tok_ahead - vocab0
    peak = jnp.max(logits, axis=0, keepdims=True)
    ex = jnp.exp(logits - peak)
    e_own[...] = ex
    rest = jnp.where(hit, 0.0, ex)
    total = jnp.sum(rest, axis=0, keepdims=True)
    picked = jnp.sum(jnp.where(hit, logits, 0.0), axis=0, keepdims=True)

    def merge(buf, n):
        m = buf[0, 0:1, :]
        for i in range(1, n):
            m = jnp.maximum(m, buf[i, 0:1, :])
        s, p = jnp.zeros_like(m), jnp.zeros_like(m)
        for i in range(n):
            s += buf[i, 1:2, :] * jnp.exp(buf[i, 0:1, :] - m)
            p += buf[i, 2:3, :]
        return m, s, p

    def put(buf, idx, m, s, p):
        buf[idx, 0:1, :] = m
        buf[idx, 1:2, :] = s
        buf[idx, 2:3, :] = p
        buf[idx, 3:8, :] = jnp.zeros((5, TOKENS), F32)

    eb[j] = lax.dot_general(
        perm.astype(BF16), rest.astype(BF16), (((1,), (1,)), ((), ())), preferred_element_type=F32
    ).astype(BF16)
    put(stx, j, peak, total, picked)
    for dj in range(1, 8):
        send(stx.at[j], stx.at[j], xs.at[dj], xr.at[j], dev(lax.rem(j + dj, 8), y, z))
    for dj in range(1, 8):
        send(eb.at[j], eb.at[j], es.at[dj], er.at[j], dev(lax.rem(j + dj, 8), y, z))

    for jj in range(8):
        recv(wg.at[jj], ws.at[0], wr.at[jj], jj != j)
    lane = lax.broadcasted_iota(jnp.int32, (TOKENS, 8 * VROWS), 1)
    one = (lane == ahead_col - (pipe * 32 + h * 8) * VROWS).astype(F32).astype(BF16)
    w_all = wg[...].reshape(8 * VROWS, PIECE)
    hb[...] = jnp.dot(one, w_all, preferred_element_type=F32).astype(BF16).reshape(12, 16, PIECE)
    for dz in range(1, 12):
        tz = lax.rem(z + dz, 12)
        send(hb.at[tz], rh.at[z], rhss.at[dz], rhrs.at[z], dev(j, y, tz))

    for jj in range(8):
        recv(stx.at[jj], xs.at[0], xr.at[jj], jj != j)
    mx, sx, px = merge(stx, 8)
    put(sty, y, mx, sx, px)
    for dy in range(1, 8):
        send(sty.at[y], sty.at[y], tys.at[dy], tyr.at[y], dev(j, lax.rem(y + dy, 8), z))

    for jj in range(8):
        st[jj:jj + 1, :] = jnp.exp(stx[jj, 0:1, :] - mx)
    cols = columns(st[0:8, :])
    for jj in range(8):
        recv(eb.at[jj], es.at[0], er.at[jj], jj != j)
        lgb[:, jj * VROWS:(jj + 1) * VROWS] = (cols[:, jj:jj + 1] * eb[jj].astype(F32)).astype(BF16)
    part = jnp.dot(lgb[...], w_all, preferred_element_type=F32)
    pf[...] = part.reshape(8, 24, PIECE)
    pb[...] = pf[...].astype(BF16)
    for dy in range(1, 8):
        ty = lax.rem(y + dy, 8)
        send(pb.at[ty], r1.at[y], r1ss.at[dy], r1rs.at[y], dev(j, ty, z))

    for yy in range(8):
        recv(sty.at[yy], tys.at[0], tyr.at[yy], yy != y)
    my, sy, py = merge(sty, 8)
    put(stz, z, my, sy, py)
    for dz in range(1, 12):
        send(stz.at[z], stz.at[z], tzs.at[dz], tzr.at[z], dev(j, y, lax.rem(z + dz, 12)))
    for yy in range(8):
        st[yy:yy + 1, :] = jnp.exp(sty[yy, 0:1, :] - my)
    row24 = lax.broadcasted_iota(jnp.int32, (24, TOKENS), 0)
    six24 = lax.shift_right_logical(row24 * 10923, 16)
    pick24 = lax.broadcasted_iota(jnp.int32, (24, TOKENS), 1) == six24 * 48 + y * 6 + (row24 - six24 * 6)
    cols_y = columns(st[0:8, :], pick24.astype(F32))

    for zz in range(12):
        recv(stz.at[zz], tzs.at[0], tzr.at[zz], zz != z)
    m_all, s_rest, picked_all = merge(stz, 12)
    s_all = s_rest + jnp.exp(picked_all - m_all)
    log_total = m_all + jnp.log(s_all)
    loss[...] = jnp.sum(weight * (log_total - picked_all), axis=1, keepdims=True)
    for zz in range(12):
        st[zz:zz + 1, :] = scaled * jnp.exp(stz[zz, 0:1, :] - log_total)
    st[12:13, :] = (scaled * (s_rest / s_all)).astype(BF16).astype(F32)
    st[13:16, :] = jnp.zeros((3, TOKENS), F32)
    first = h * 48 + y * 6 + 2 * lo
    pick2 = (
        lax.broadcasted_iota(jnp.int32, (8, TOKENS), 1)
        == lax.broadcasted_iota(jnp.int32, (8, TOKENS), 0) + first
    )
    cols_z = columns(st[...], pick2.astype(F32))

    probs = (scaled * (e_own[...] * jnp.exp(peak - log_total))).astype(BF16)
    for p in range(8):
        wgs[:, p * PIECE:(p + 1) * PIECE] = jnp.dot(
            probs, hp[p].reshape(TOKENS, PIECE), preferred_element_type=F32
        ).astype(BF16)
    out = pltpu.make_async_copy(wgs, wgrad, outsem)
    out.start()

    rh[z] = hb[z]
    hsum[...] = jnp.zeros((16, PIECE), F32)
    for zz in range(12):
        recv(rh.at[zz], rhss.at[0], rhrs.at[zz], zz != z)
        hsum[...] += rh[zz].astype(F32)
    for yy in range(8):
        h2s[yy] = hsum[2 * yy:2 * yy + 2, :].astype(BF16)
    for dy in range(1, 8):
        ty = lax.rem(y + dy, 8)
        send(h2s.at[ty], h2.at[y], h2ss.at[dy], h2rs.at[y], dev(j, ty, z))

    r1[y] = jnp.zeros((24, PIECE), BF16)
    tot = pf[y] * jnp.sum(
        jnp.where(lax.broadcasted_iota(jnp.int32, (24, 8), 1) == y, cols_y, 0.0), axis=1, keepdims=True
    )
    for yy in range(8):
        recv(r1.at[yy], r1ss.at[0], r1rs.at[yy], yy != y)
        tot += cols_y[:, yy:yy + 1] * r1[yy].astype(F32)
    for zz in range(12):
        r2s[zz] = tot[2 * zz:2 * zz + 2, :].astype(BF16)
    for dz in range(1, 12):
        tz = lax.rem(z + dz, 12)
        send(r2s.at[tz], r2.at[z], r2ss.at[dz], r2rs.at[z], dev(j, y, tz))
    r2[z] = r2s[z]
    h2[y] = h2s[y]
    target = jnp.zeros((2, PIECE), F32)
    for yy in range(8):
        recv(h2.at[yy], h2ss.at[0], h2rs.at[yy], yy != y)
        target += h2[yy].astype(F32)
    fin = -cols_z[0:2, 12:13] * target
    for zz in range(12):
        recv(r2.at[zz], r2ss.at[0], r2rs.at[zz], zz != z)
        fin += cols_z[0:2, zz:zz + 1] * r2[zz].astype(F32)
    gs[...] = fin.astype(BF16)

    for l3 in range(3):
        for yy in range(8):
            to = dev(y, yy, h * 3 + l3)
            away = jnp.logical_or(jnp.logical_or(j != y, yy != y), lo != l3)
            send(gs, gb.at[lo, j], gss.at[l3, yy], grs.at[lo, j], to, away)

    @pl.when(j == y)
    def _():
        gb[lo, j] = gs[...]

    for l3 in range(3):
        for jj in range(8):
            away = jnp.logical_or(jnp.logical_or(j != y, jj != j), lo != l3)
            recv(gb.at[l3, jj], gss.at[0, 0], grs.at[l3, jj], away)
            rowf[2 * l3:2 * l3 + 2, jj * PIECE:(jj + 1) * PIECE] = gb[l3, jj].astype(F32)
    rowg[...] = rowf[0:6, :].astype(BF16)

    for d, cond in sends:
        if cond is None:
            d.wait_send()
        else:
            pl.when(cond)(d.wait_send)
    out.wait()


W_FIRST = (1, 2, 3, 4, 5, 6, 7)
W_LATER = ((), (), (), ())


def body(hidden, head_weight, token_ids, segment_ids):
    dma = pltpu.SemaphoreType.DMA
    vmem = pl.BlockSpec(memory_space=pltpu.VMEM)
    hbm = pl.BlockSpec(memory_space=pltpu.HBM)
    row_grad, weight_grad, target_rows, loss = pl.pallas_call(
        kernel,
        out_shape=(
            jax.ShapeDtypeStruct((6, WIDTH), BF16),
            jax.ShapeDtypeStruct((VROWS, WIDTH), BF16),
            jax.ShapeDtypeStruct((6, WIDTH), BF16),
            jax.ShapeDtypeStruct((1, 1), F32),
        ),
        in_specs=[hbm, hbm, vmem, vmem],
        out_specs=(vmem, hbm, vmem, vmem),
        scratch_shapes=[
            pltpu.VMEM((6, WIDTH), BF16),
            pltpu.VMEM((VROWS, WIDTH), BF16),
            pltpu.VMEM((8, 6, PIECE), BF16),
            pltpu.VMEM((48, PIECE), F32),
            pltpu.VMEM((8, 4, 48, PIECE), BF16),
            pltpu.VMEM((8, VROWS, PIECE), BF16),
            pltpu.VMEM((VROWS, TOKENS), F32),
            pltpu.VMEM((VROWS, TOKENS), F32),
            pltpu.VMEM((16, TOKENS), F32),
            pltpu.VMEM((8, 8, TOKENS), F32),
            pltpu.VMEM((8, 8, TOKENS), F32),
            pltpu.VMEM((12, 8, TOKENS), F32),
            pltpu.VMEM((8, TOKENS, VROWS), BF16),
            pltpu.VMEM((TOKENS, 8 * VROWS), BF16),
            pltpu.VMEM((8, 24, PIECE), F32),
            pltpu.VMEM((8, 24, PIECE), BF16),
            pltpu.VMEM((12, 16, PIECE), BF16),
            pltpu.VMEM((8, 24, PIECE), BF16),
            pltpu.VMEM((12, 16, PIECE), BF16),
            pltpu.VMEM((16, PIECE), F32),
            pltpu.VMEM((8, 2, PIECE), BF16),
            pltpu.VMEM((8, 2, PIECE), BF16),
            pltpu.VMEM((12, 2, PIECE), BF16),
            pltpu.VMEM((12, 2, PIECE), BF16),
            pltpu.VMEM((2, PIECE), BF16),
            pltpu.VMEM((3, 8, 2, PIECE), BF16),
            pltpu.VMEM((8, WIDTH), F32),
            pltpu.VMEM((VROWS, WIDTH), BF16),
            dma((2,)), dma((4,)), dma((4,)), dma((8,)), dma((8,)), dma((8,)),
            dma((2, 4)), dma((2, 4)), dma((8,)), dma((8,)), dma((8,)), dma((8, 2)), dma((8, 2)),
            dma((8,)), dma((8,)), dma((8,)), dma((8,)), dma((8,)), dma((8,)), dma((12,)), dma((12,)),
            dma((8,)), dma((8,)), dma((12,)), dma((12,)), dma((8,)), dma((8,)), dma((12,)), dma((12,)),
            dma((3, 8)), dma((3, 8)), dma,
        ],
        compiler_params=pltpu.CompilerParams(
            collective_id=0, has_side_effects=True, vmem_limit_bytes=56 * 2**20
        ),
    )(hidden, head_weight, token_ids.reshape(1, TOKENS), segment_ids.reshape(1, TOKENS))
    return (row_grad, weight_grad, target_rows, loss.reshape(()))


def solution(mesh):
    placed = (P("dp", None), P(("pipe", "dp"), None), P(), P())
    return jax.shard_map(
        body,
        mesh=mesh,
        in_specs=placed,
        out_specs=(P("dp", None), P(("pipe", "dp"), None), P("dp", None), P()),
        check_vma=False,
    )
```

```python
import functools

import jax
import jax.numpy as jnp
from jax import lax
from jax.experimental import pallas as pl
from jax.experimental.pallas import tpu as pltpu
from jax.sharding import PartitionSpec as P

MESH = pl.DeviceIdType.MESH
LOSS_SCALE = 4096.0
TURNS = 16
TOKENS = 192
WIDTH = 7168
PIECE = 896
VROWS = 128
BF16 = jnp.bfloat16
F32 = jnp.float32


def kernel(
    hid, w_hbm, tok_in, seg_in,
    rowg, wgrad, trow, loss,
    hidv, w_ref, sbuf, scr48, hp, wg, acc, e_own, st, stx, sty, stz, eb, lgb, pf, pb, hb, r1, rh, hsum, h2s, h2,
    r2s, r2, gs, gb, rowf, wgs,
    lsem, ss0, ss1, sr, ws, wr, ys, yr, zus, zds, zr, cs, cr, xs, xr, es, er, tys, tyr, tzs, tzr,
    r1ss, r1rs, rhss, rhrs, h2ss, h2rs, r2ss, r2rs, gss, grs, outsem,
):
    pipe, dp = lax.axis_index("pipe"), lax.axis_index("dp")
    lo, y = pipe // 8, lax.rem(pipe, 8)
    h, j = dp // 8, lax.rem(dp, 8)
    x, c = j // 2, lax.rem(j, 2)
    z = h * 3 + lo

    def dev(jj, yy, zz):
        return (lax.rem(zz, 3) * 8 + yy, (zz // 3) * 8 + jj)

    sends = []

    def send(src, dst, ss, rs, to, cond=None):
        d = pltpu.make_async_remote_copy(
            src_ref=src, dst_ref=dst, send_sem=ss, recv_sem=rs, device_id=to, device_id_type=MESH
        )
        if cond is None:
            d.start()
        else:
            pl.when(cond)(d.start)
        sends.append((d, cond))

    def flush(keep=0):
        while len(sends) > keep:
            d, cond = sends.pop(0)
            if cond is None:
                d.wait_send()
            else:
                pl.when(cond)(d.wait_send)

    def recv(dst, ss, rs, cond=None):
        d = pltpu.make_async_remote_copy(
            src_ref=dst, dst_ref=dst, send_sem=ss, recv_sem=rs,
            device_id=dev(j, lax.rem(y + 1, 8), z), device_id_type=MESH,
        )
        if cond is None:
            d.wait_recv()
        else:
            pl.when(cond)(d.wait_recv)

    loads = [
        pltpu.make_async_copy(a, b, lsem.at[i])
        for i, (a, b) in enumerate(((hid, hidv), (w_hbm, w_ref)))
    ]
    bar = pltpu.get_barrier_semaphore()

    def hello(to):
        pl.semaphore_signal(bar, inc=1, device_id=to, device_id_type=MESH)

    for dz in (6, 5, 7, 4, 8, 3, 9, 2, 10, 1, 11):
        hello(dev(j, y, lax.rem(z + dz, 12)))
    for dy in (4, 3, 5, 2, 6, 1, 7):
        hello(dev(j, lax.rem(y + dy, 8), z))
    for dj in range(1, 8):
        hello(dev(lax.rem(j + dj, 8), y, z))
    near_z = jnp.where(c == 0, lax.rem(z + 11, 12), lax.rem(z + 1, 12))
    for cc in range(2):
        hello(dev(x * 2 + cc, y, near_z))
    from_z = lax.rem(z + 3 + 3 * lo, 12)

    @pl.when(c == 1)
    def _():
        for jj in range(8):
            hello(dev(jj, y, from_z))

    for d in loads:
        d.start()

    pl.semaphore_wait(bar, 25 + 2 + 4)

    col = pl.ds(pl.multiple_of(y * PIECE, 128), PIECE)
    far_z = lax.rem(z + 9 - 3 * lo, 12)
    for dx in (2, 1, 3, 0):
        tx = lax.rem(x + dx, 4)
        send(hid.at[:, col], sbuf.at[j], ss1.at[dx], sr.at[j], dev(tx * 2 + 1, y, far_z))
    for dx in (2, 1, 3, 0):
        tx = lax.rem(x + dx, 4)
        send(
            hid.at[:, col], sbuf.at[j], ss0.at[dx], sr.at[j], dev(tx * 2, y, z),
            (c != 0) if dx == 0 else None,
        )

    def send_w(dj):
        tj = lax.rem(j + dj, 8)
        send(
            w_hbm.at[:, pl.ds(pl.multiple_of(tj * PIECE, 128), PIECE)], wg.at[j],
            ws.at[dj], wr.at[j], dev(tj, y, z),
        )

    def shifted(v, fill):
        return jnp.concatenate([v[:, 2:], jnp.full((1, 2), fill, jnp.int32)], axis=1)

    tok_ahead = shifted(tok_in[...], 0)
    seg = seg_in[...]
    seg_ahead = shifted(seg, -1)
    valid = (seg_ahead == seg).astype(F32)
    member = (lax.broadcasted_iota(jnp.int32, (TURNS, TOKENS), 0) == seg).astype(F32)
    counts = jnp.sum(member * valid, axis=1, keepdims=True)
    per_token = jnp.sum(member * counts, axis=0, keepdims=True)
    weight = valid / (jnp.maximum(per_token, 1.0) * TURNS)
    scaled = LOSS_SCALE * weight
    pick6 = (
        lax.broadcasted_iota(jnp.int32, (6, TOKENS), 1)
        == lax.broadcasted_iota(jnp.int32, (6, TOKENS), 0) + dp * 6
    )
    own_scaled = jnp.sum(jnp.where(pick6, scaled, 0.0), axis=1, keepdims=True)
    row = lax.broadcasted_iota(jnp.int32, (TOKENS, TOKENS), 0)
    six = lax.shift_right_logical(row * 10923, 16)
    token_of = (six & 3) * 48 + lax.shift_right_logical(six, 2) * 6 + (row - six * 6)
    perm = (lax.broadcasted_iota(jnp.int32, (TOKENS, TOKENS), 1) == token_of).astype(F32)

    def columns(rows, order=perm):
        return lax.dot_general(
            order, rows, (((1,), (1,)), ((), ())),
            preferred_element_type=F32, precision=lax.Precision.HIGHEST,
        )

    st[0:8, :] = jnp.broadcast_to(tok_ahead.astype(F32), (8, TOKENS))
    zed = lax.shift_right_logical(row, 4)
    third = lax.shift_right_logical(zed * 21846, 16)
    token_of = third * 48 + (lax.shift_right_logical(row, 1) & 7) * 6 + (zed - third * 3) * 2 + (row & 1)
    order = (lax.broadcasted_iota(jnp.int32, (TOKENS, TOKENS), 1) == token_of).astype(F32)
    ahead_col = jnp.round(columns(st[0:8, :], order)[:, 0:1]).astype(jnp.int32)
    loads[0].wait()
    trow[...] = (-own_scaled * hidv[...].astype(F32)).astype(BF16)

    loads[1].wait()
    wg[j] = w_ref[:, pl.ds(pl.multiple_of(j * PIECE, 128), PIECE)]

    @pl.when(c == 0)
    def _():
        sbuf[j] = hidv[:, col]

    for jj in range(8):
        recv(sbuf.at[jj], ss0.at[0], sr.at[jj], jnp.logical_or(jj != j, c == 1))
    for jj in range(8):
        scr48[6 * jj:6 * jj + 6, :] = sbuf[jj].astype(F32)
    ring_of = (h, lax.rem(h + 1 + lo, 4))
    zed_of = (
        lax.rem(h + jnp.where(lo == 0, 3, lo), 4),
        lax.rem(h + jnp.where(lo == 2, 1, lo + 2), 4),
    )

    def mine(pair):
        return jnp.where(c == 0, pair[0], pair[1])

    def other(pair):
        return jnp.where(c == 0, pair[1], pair[0])

    ring_b, zed_b, sib_ring, sib_zed = mine(ring_of), mine(zed_of), other(ring_of), other(zed_of)
    hp[y, ring_b] = scr48[...].astype(BF16)

    right, left = dev(j, lax.rem(y + 1, 8), z), dev(j, lax.rem(y + 7, 8), z)
    above, below = dev(x * 2, y, lax.rem(z + 1, 12)), dev(x * 2 + 1, y, lax.rem(z + 11, 12))
    sib = dev(x * 2 + 1 - c, y, z)
    sends_up = c == jnp.where(lo < 2, 1, 0)
    sends_down = c == jnp.where(lo > 0, 1, 0)

    def slot(k, way):
        return 0 if k == 0 else (7 if k == 4 else 1 + 2 * (k - 1) + way)

    def piece(k, way):
        return y if k == 0 else lax.rem(y + (8 - k if way == 0 else k), 8)

    def part_of(k, way, sub):
        return hp.at[piece(k, way), ring_b, :, pl.ds(*SUBS[sub])]

    def ring_on(k, way, sub):
        blk = part_of(k, way, sub)
        for w in (0, 1):
            if (k == 0 or w == way) and k < 4:
                send(
                    blk, blk, ys.at[w, k, sub], yr.at[w, k, sub], right if w == 0 else left,
                    (c == w) if k == 3 else None,
                )

    def pass_on(k, way):
        n = slot(k, way)
        blk = hp.at[piece(k, way), ring_b]
        send(blk, blk, zus.at[n], zr.at[n], above, sends_up)
        send(blk, blk, zds.at[n], zr.at[n], below, sends_down)
        send(blk, blk, cs.at[n, 0], cr.at[n, 0], sib)

    def zed_on(k, way):
        n = slot(k, way)
        blk = hp.at[piece(k, way), zed_b]
        recv(blk, zus.at[n], zr.at[n])
        send(blk, blk, cs.at[n, 1], cr.at[n, 1], sib)

    def logits_of(k, way):
        n, p = slot(k, way), piece(k, way)
        recv(hp.at[p, sib_ring], cs.at[n, 0], cr.at[n, 0])
        recv(hp.at[p, sib_zed], cs.at[n, 1], cr.at[n, 1])
        tile = w_ref[:, pl.ds(pl.multiple_of(p * PIECE, 128), PIECE)]
        tokens = hp[p].reshape(TOKENS, PIECE)
        part = lax.dot_general(tile, tokens, (((1,), (1,)), ((), ())), preferred_element_type=F32)
        if k == 0:
            acc[...] = part
        else:
            acc[...] += part

    def ways(k):
        return (0,) if k in (0, 4) else (0, 1)

    for sub in (0, 1):
        ring_on(0, 0, sub)
    pass_on(0, 0)
    for dj in W_FIRST:
        send_w(dj)
    for k in range(1, 5):
        if k == 4:
            for sub in (0, 1):
                recv(part_of(4, 0, sub), ys.at[c, 3, sub], yr.at[c, 3, sub])
            pass_on(4, 0)
        else:
            for sub in (0, 1):
                for way in (0, 1):
                    recv(part_of(k, way, sub), ys.at[way, k - 1, sub], yr.at[way, k - 1, sub])
                    ring_on(k, way, sub)
            for way in (0, 1):
                pass_on(k, way)
        for dj in W_LATER[k - 1]:
            send_w(dj)
        for way in ways(k - 1):
            zed_on(k - 1, way)
        if k >= 2:
            for way in ways(k - 2):
                logits_of(k - 2, way)
    zed_on(4, 0)
    for way in ways(3):
        logits_of(3, way)
    logits_of(4, 0)

    logits = acc[...]
    vocab0 = (pipe * 32 + dp) * VROWS
    hit = lax.broadcasted_iota(jnp.int32, (VROWS, TOKENS), 0) == tok_ahead - vocab0
    peak = jnp.max(logits, axis=0, keepdims=True)
    ex = jnp.exp(logits - peak)
    e_own[...] = ex
    rest = jnp.where(hit, 0.0, ex)
    total = jnp.sum(rest, axis=0, keepdims=True)
    picked = jnp.sum(jnp.where(hit, logits, 0.0), axis=0, keepdims=True)

    def merge(buf, n):
        m = buf[0, 0:1, :]
        for i in range(1, n):
            m = jnp.maximum(m, buf[i, 0:1, :])
        s, p = jnp.zeros_like(m), jnp.zeros_like(m)
        for i in range(n):
            s += buf[i, 1:2, :] * jnp.exp(buf[i, 0:1, :] - m)
            p += buf[i, 2:3, :]
        return m, s, p

    def put(buf, idx, m, s, p):
        buf[idx, 0:1, :] = m
        buf[idx, 1:2, :] = s
        buf[idx, 2:3, :] = p
        buf[idx, 3:8, :] = jnp.zeros((5, TOKENS), F32)

    eb[j] = lax.dot_general(
        perm.astype(BF16), rest.astype(BF16), (((1,), (1,)), ((), ())), preferred_element_type=F32
    ).astype(BF16)
    put(stx, j, peak, total, picked)
    for dj in range(1, 8):
        send(stx.at[j], stx.at[j], xs.at[dj], xr.at[j], dev(lax.rem(j + dj, 8), y, z))
    for dj in range(1, 8):
        send(eb.at[j], eb.at[j], es.at[dj], er.at[j], dev(lax.rem(j + dj, 8), y, z))

    for jj in range(8):
        recv(wg.at[jj], ws.at[0], wr.at[jj], jj != j)
    lane = lax.broadcasted_iota(jnp.int32, (TOKENS, 8 * VROWS), 1)
    one = (lane == ahead_col - (pipe * 32 + h * 8) * VROWS).astype(F32).astype(BF16)
    w_all = wg[...].reshape(8 * VROWS, PIECE)
    hb[...] = jnp.dot(one, w_all, preferred_element_type=F32).astype(BF16).reshape(12, 16, PIECE)
    for dz in range(1, 12):
        tz = lax.rem(z + dz, 12)
        send(hb.at[tz], rh.at[z], rhss.at[dz], rhrs.at[z], dev(j, y, tz))

    for jj in range(8):
        recv(stx.at[jj], xs.at[0], xr.at[jj], jj != j)
    mx, sx, px = merge(stx, 8)
    put(sty, y, mx, sx, px)
    for dy in range(1, 8):
        send(sty.at[y], sty.at[y], tys.at[dy], tyr.at[y], dev(j, lax.rem(y + dy, 8), z))

    for jj in range(8):
        st[jj:jj + 1, :] = jnp.exp(stx[jj, 0:1, :] - mx)
    cols = columns(st[0:8, :])
    for jj in range(8):
        recv(eb.at[jj], es.at[0], er.at[jj], jj != j)
        lgb[:, jj * VROWS:(jj + 1) * VROWS] = (cols[:, jj:jj + 1] * eb[jj].astype(F32)).astype(BF16)
    part = jnp.dot(lgb[...], w_all, preferred_element_type=F32)
    pf[...] = part.reshape(8, 24, PIECE)
    pb[...] = pf[...].astype(BF16)
    for dy in range(1, 8):
        ty = lax.rem(y + dy, 8)
        send(pb.at[ty], r1.at[y], r1ss.at[dy], r1rs.at[y], dev(j, ty, z))

    for yy in range(8):
        recv(sty.at[yy], tys.at[0], tyr.at[yy], yy != y)
    my, sy, py = merge(sty, 8)
    put(stz, z, my, sy, py)
    for dz in range(1, 12):
        send(stz.at[z], stz.at[z], tzs.at[dz], tzr.at[z], dev(j, y, lax.rem(z + dz, 12)))
    for yy in range(8):
        st[yy:yy + 1, :] = jnp.exp(sty[yy, 0:1, :] - my)
    row24 = lax.broadcasted_iota(jnp.int32, (24, TOKENS), 0)
    six24 = lax.shift_right_logical(row24 * 10923, 16)
    pick24 = lax.broadcasted_iota(jnp.int32, (24, TOKENS), 1) == six24 * 48 + y * 6 + (row24 - six24 * 6)
    cols_y = columns(st[0:8, :], pick24.astype(F32))

    rh[z] = hb[z]
    hsum[...] = jnp.zeros((16, PIECE), F32)
    for zz in range(12):
        recv(rh.at[zz], rhss.at[0], rhrs.at[zz], zz != z)
        hsum[...] += rh[zz].astype(F32)
    for yy in range(8):
        h2s[yy] = hsum[2 * yy:2 * yy + 2, :].astype(BF16)
    for dy in range(1, 8):
        ty = lax.rem(y + dy, 8)
        send(h2s.at[ty], h2.at[y], h2ss.at[dy], h2rs.at[y], dev(j, ty, z))

    r1[y] = jnp.zeros((24, PIECE), BF16)
    tot = pf[y] * jnp.sum(
        jnp.where(lax.broadcasted_iota(jnp.int32, (24, 8), 1) == y, cols_y, 0.0), axis=1, keepdims=True
    )
    for yy in range(8):
        recv(r1.at[yy], r1ss.at[0], r1rs.at[yy], yy != y)
        tot += cols_y[:, yy:yy + 1] * r1[yy].astype(F32)
    for zz in range(12):
        r2s[zz] = tot[2 * zz:2 * zz + 2, :].astype(BF16)
    for dz in range(1, 12):
        tz = lax.rem(z + dz, 12)
        send(r2s.at[tz], r2.at[z], r2ss.at[dz], r2rs.at[z], dev(j, y, tz))
    for zz in range(12):
        recv(stz.at[zz], tzs.at[0], tzr.at[zz], zz != z)
    m_all, s_rest, picked_all = merge(stz, 12)
    s_all = s_rest + jnp.exp(picked_all - m_all)
    log_total = m_all + jnp.log(s_all)
    loss[...] = jnp.sum(weight * (log_total - picked_all), axis=1, keepdims=True)
    for zz in range(12):
        st[zz:zz + 1, :] = scaled * jnp.exp(stz[zz, 0:1, :] - log_total)
    st[12:13, :] = (scaled * (s_rest / s_all)).astype(BF16).astype(F32)
    st[13:16, :] = jnp.zeros((3, TOKENS), F32)
    first = h * 48 + y * 6 + 2 * lo
    pick2 = (
        lax.broadcasted_iota(jnp.int32, (8, TOKENS), 1)
        == lax.broadcasted_iota(jnp.int32, (8, TOKENS), 0) + first
    )
    cols_z = columns(st[...], pick2.astype(F32))

    probs = (scaled * (e_own[...] * jnp.exp(peak - log_total))).astype(BF16)

    def one_piece(p, carry):
        wgs[:, pl.ds(pl.multiple_of(p * PIECE, 128), PIECE)] = jnp.dot(
            probs, hp[p].reshape(TOKENS, PIECE), preferred_element_type=F32
        ).astype(BF16)
        return carry

    lax.fori_loop(0, 8, one_piece, 0)
    out = pltpu.make_async_copy(wgs, wgrad, outsem)
    out.start()

    r2[z] = r2s[z]
    h2[y] = h2s[y]
    target = jnp.zeros((2, PIECE), F32)
    for yy in range(8):
        recv(h2.at[yy], h2ss.at[0], h2rs.at[yy], yy != y)
        target += h2[yy].astype(F32)
    fin = -cols_z[0:2, 12:13] * target
    for zz in range(12):
        recv(r2.at[zz], r2ss.at[0], r2rs.at[zz], zz != z)
        fin += cols_z[0:2, zz:zz + 1] * r2[zz].astype(F32)
    gs[...] = fin.astype(BF16)

    for l3 in range(3):
        for yy in range(8):
            to = dev(y, yy, h * 3 + l3)
            away = jnp.logical_or(jnp.logical_or(j != y, yy != y), lo != l3)
            send(gs, gb.at[lo, j], gss.at[l3, yy], grs.at[lo, j], to, away)

    @pl.when(j == y)
    def _():
        gb[lo, j] = gs[...]

    flush(24)
    for l3 in range(3):
        for jj in range(8):
            away = jnp.logical_or(jnp.logical_or(j != y, jj != j), lo != l3)
            recv(gb.at[l3, jj], gss.at[0, 0], grs.at[l3, jj], away)
            rowf[2 * l3:2 * l3 + 2, jj * PIECE:(jj + 1) * PIECE] = gb[l3, jj].astype(F32)
    rowg[...] = rowf[0:6, :].astype(BF16)

    flush()
    out.wait()


SUBS = ((0, 512), (512, 384))
W_FIRST = (1, 2, 3, 4, 5, 6, 7)
W_LATER = ((), (), (), ())


def body(hidden, head_weight, token_ids, segment_ids):
    dma = pltpu.SemaphoreType.DMA
    vmem = pl.BlockSpec(memory_space=pltpu.VMEM)
    hbm = pl.BlockSpec(memory_space=pltpu.HBM)
    row_grad, weight_grad, target_rows, loss = pl.pallas_call(
        kernel,
        out_shape=(
            jax.ShapeDtypeStruct((6, WIDTH), BF16),
            jax.ShapeDtypeStruct((VROWS, WIDTH), BF16),
            jax.ShapeDtypeStruct((6, WIDTH), BF16),
            jax.ShapeDtypeStruct((1, 1), F32),
        ),
        in_specs=[hbm, hbm, vmem, vmem],
        out_specs=(vmem, hbm, vmem, vmem),
        scratch_shapes=[
            pltpu.VMEM((6, WIDTH), BF16),
            pltpu.VMEM((VROWS, WIDTH), BF16),
            pltpu.VMEM((8, 6, PIECE), BF16),
            pltpu.VMEM((48, PIECE), F32),
            pltpu.VMEM((8, 4, 48, PIECE), BF16),
            pltpu.VMEM((8, VROWS, PIECE), BF16),
            pltpu.VMEM((VROWS, TOKENS), F32),
            pltpu.VMEM((VROWS, TOKENS), F32),
            pltpu.VMEM((16, TOKENS), F32),
            pltpu.VMEM((8, 8, TOKENS), F32),
            pltpu.VMEM((8, 8, TOKENS), F32),
            pltpu.VMEM((12, 8, TOKENS), F32),
            pltpu.VMEM((8, TOKENS, VROWS), BF16),
            pltpu.VMEM((TOKENS, 8 * VROWS), BF16),
            pltpu.VMEM((8, 24, PIECE), F32),
            pltpu.VMEM((8, 24, PIECE), BF16),
            pltpu.VMEM((12, 16, PIECE), BF16),
            pltpu.VMEM((8, 24, PIECE), BF16),
            pltpu.VMEM((12, 16, PIECE), BF16),
            pltpu.VMEM((16, PIECE), F32),
            pltpu.VMEM((8, 2, PIECE), BF16),
            pltpu.VMEM((8, 2, PIECE), BF16),
            pltpu.VMEM((12, 2, PIECE), BF16),
            pltpu.VMEM((12, 2, PIECE), BF16),
            pltpu.VMEM((2, PIECE), BF16),
            pltpu.VMEM((3, 8, 2, PIECE), BF16),
            pltpu.VMEM((8, WIDTH), F32),
            pltpu.VMEM((VROWS, WIDTH), BF16),
            dma((2,)), dma((4,)), dma((4,)), dma((8,)), dma((8,)), dma((8,)),
            dma((2, 4, 2)), dma((2, 4, 2)), dma((8,)), dma((8,)), dma((8,)), dma((8, 2)), dma((8, 2)),
            dma((8,)), dma((8,)), dma((8,)), dma((8,)), dma((8,)), dma((8,)), dma((12,)), dma((12,)),
            dma((8,)), dma((8,)), dma((12,)), dma((12,)), dma((8,)), dma((8,)), dma((12,)), dma((12,)),
            dma((3, 8)), dma((3, 8)), dma,
        ],
        compiler_params=pltpu.CompilerParams(
            collective_id=0, has_side_effects=True, vmem_limit_bytes=56 * 2**20
        ),
    )(hidden, head_weight, token_ids.reshape(1, TOKENS), segment_ids.reshape(1, TOKENS))
    return (row_grad, weight_grad, target_rows, loss.reshape(()))


def solution(mesh):
    placed = (P("dp", None), P(("pipe", "dp"), None), P(), P())
    return jax.shard_map(
        body,
        mesh=mesh,
        in_specs=placed,
        out_specs=(P("dp", None), P(("pipe", "dp"), None), P("dp", None), P()),
        check_vma=False,
    )
```
